32 devices in a mesh: dp: 8 (over z, y), tensor: 4 (over x, core).
Axes of the slice: x: 2, y: 2, z: 4, core: 2. Of those that a mesh axis runs over, the one named last changes fastest.
Arguments:
- hidden_in: bfloat16 [8192, 2048], P(('dp', 'tensor')), may hold values from -6 to 6
- layer_input: bfloat16 [8192, 256], P(('dp', 'tensor')), may hold values from -6 to 6
- cached_len: int32 [16], replicated, may hold values from 3584 to 4096, as said below
- page_table: int32 [16, 32], replicated, may hold values from 0 to 511, as said below
- kv_pool: bfloat16 [512, 2, 2, 128, 256], P(('dp', 'tensor'))
- norm_in: float32 [2048], replicated, may hold values from 0.5 to 1.5
- w_query: bfloat16 [2048, 2048], P(None, 'tensor'), may hold values from -0.125 to 0.125
- w_keyval: bfloat16 [2048, 1024], replicated, may hold values from -0.125 to 0.125
- q_gain: float32 [256], replicated, may hold values from 0.1 to 0.4
- k_gain: float32 [256], replicated, may hold values from 0.5 to 1.5
- w_out: bfloat16 [2048, 2048], P('tensor'), may hold values from -0.125 to 0.125
- post_attn_gain: float32 [2048], replicated, may hold values from 0.5 to 1.5
- laurel_left: bfloat16 [2048, 64], replicated, may hold values from -0.125 to 0.125
- laurel_right: bfloat16 [64, 2048], replicated, may hold values from -0.75 to 0.75
- laurel_gain: float32 [2048], replicated, may hold values from 0.5 to 1.5
- pre_ffn_gain: float32 [2048], replicated, may hold values from 0.5 to 1.5
- w_gate: bfloat16 [2048, 8192], P(None, 'tensor'), may hold values from -0.125 to 0.125
- w_up: bfloat16 [2048, 8192], P(None, 'tensor'), may hold values from -0.125 to 0.125
- w_down: bfloat16 [8192, 2048], P('tensor'), may hold values from -0.0625 to 0.0625
- post_ffn_gain: float32 [2048], replicated, may hold values from 0.5 to 1.5
- ple_gate: bfloat16 [2048, 256], replicated, may hold values from -0.125 to 0.125
- ple_proj: bfloat16 [256, 2048], replicated, may hold values from -0.375 to 0.375
- ple_gain: float32 [2048], replicated, may hold values from 0.5 to 1.5
Outputs:
- layer_out: bfloat16 [8192, 2048], P(('dp', 'tensor'))
The draws below stay inside these ranges and needn't reach their ends.
Inputs may be any that keep to these rules, and one draw needn't show every extreme that they name: `cached_len`: the last request of the first index of dp, and the last request of all, have 4096 cached tokens. `page_table`: page id q lives on the device with flat index q // 16 over dp+tensor (dp slowest), at row q % 16 of its shard. Only slots below ceil(cached_len / 128) are read; every slot names a page. Requests r with the same r // 8 name the same pages in their first 8 slots, and no other page is named twice. The slots that are read by the requests of one index of dp name at most 2 distinct pages of any one device, and some index of dp reaches 2.
All inputs are finite; a program needn't handle non-finite values.
Results may differ from the reference program's by a relative error of at most 0.015.
The reference program's roundings to bfloat16 on the way count: a program that leaves them out, or rounds other values in their place, can miss the bound.
Values may be sent and summed in bfloat16 or wider, within the bound.
A program may use at most 192 MiB of HBM per device.

```python
import math
import jax
import jax.numpy as jnp
from jax import lax

D = 2048
H = 8
KVH = 2
HD = 256
FF = 8192
RANK = 64
PLE = 256
PAGE = 128
MAXCTX = 4096
PROMPT_PAGES = 8
NEW = 512
GROUP = 8
REQ_DEV = 2
SLOTS = 32
REQUESTS = 16
TOKENS = 8192
NEED = 56
CAP = 2
POOL_DEV = 16
POOLS = 512
DEVICES = 32


def pin_value(order, place, value):
    where_now = jnp.argmax(order == value).astype(jnp.int32)
    current = order[place]
    order = order.at[where_now].set(current)
    return order.at[place].set(value)


def layout_tables(key):
    base_key = jax.random.fold_in(key, 4242)
    lowest = max(PROMPT_PAGES * PAGE, MAXCTX * 7 // 8)
    lengths = jax.random.randint(jax.random.fold_in(base_key, 1), (REQUESTS,), lowest, MAXCTX + 1, dtype=jnp.int32)
    lengths = lengths.at[REQ_DEV - 1].set(MAXCTX)
    lengths = lengths.at[REQUESTS - 1].set(MAXCTX)
    group_count = REQUESTS // GROUP
    spread = GROUP // REQ_DEV
    group_keys = jax.random.split(jax.random.fold_in(base_key, 2), group_count)

    def one_order(one_key):
        order = jax.random.permutation(one_key, DEVICES).astype(jnp.int32)
        order = pin_value(order, 0, 0)
        return pin_value(order, (NEED - 1) % DEVICES, DEVICES - 1)
    orders = jax.vmap(one_order)(group_keys).astype(jnp.int32)
    request = jnp.arange(REQUESTS, dtype=jnp.int32)[:, None]
    slot_index = jnp.arange(SLOTS, dtype=jnp.int32)[None, :]
    group_of = request // GROUP
    region_of = request // REQ_DEV % spread
    member = request % REQ_DEV
    index = jnp.where(slot_index < PROMPT_PAGES, slot_index, PROMPT_PAGES + member * (SLOTS - PROMPT_PAGES) + slot_index - PROMPT_PAGES)
    region = jnp.where(slot_index < PROMPT_PAGES, 0, region_of)
    owners = jnp.take_along_axis(orders[group_of[:, 0]], index % DEVICES, axis=1)
    local_row = (spread * group_of + region) * CAP + index // DEVICES
    return (lengths, (owners * POOL_DEV + local_row).astype(jnp.int32))


def draw_cached_len(key, part):
    return layout_tables(key)[0]


def draw_page_table(key, part):
    return layout_tables(key)[1]


def draw_kv_pool(key, part):
    shape = (POOLS, 2, KVH, PAGE, HD)
    base = jax.random.normal(jax.random.fold_in(key, 11), shape, jnp.float32)
    return jnp.clip(base, -6.0, 6.0).astype(jnp.bfloat16)


def steps_of(rng, extent, cuts, low, largest):
    def one(dim, shards_of):
        steps = jax.random.uniform(jax.random.fold_in(jax.random.fold_in(rng, 6), dim), (shards_of,), jnp.float32, low / len(cuts), largest / len(cuts))
        return jnp.repeat(jnp.exp(steps), extent[dim] // shards_of).reshape((-1,) + (1,) * (len(extent) - dim - 1))

    level = one(*cuts[0])
    for cut in cuts[1:]:
        level = level * one(*cut)
    return level


def bell_draw(rng, dims, scale, most, pieces=(), held_as=jnp.bfloat16):
    result = scale * jax.random.normal(rng, dims, jnp.float32)
    if pieces:
        result = result * steps_of(rng, dims, pieces, -0.22, 0.18)
    return jnp.clip(result, -most, most).astype(held_as)


def setup_inputs(seed: int = 0) -> dict:
    splits = jax.random.split(jax.random.key(seed), 24)
    hidden_in = bell_draw(splits[0], (TOKENS, D), 1.0, 6.0, ((0, 32),))
    layer_input = bell_draw(splits[1], (TOKENS, PLE), 1.0, 6.0, ((0, 32),))
    cached_len = draw_cached_len(jax.random.fold_in(splits[23], 71), 0)
    page_table = draw_page_table(jax.random.fold_in(splits[23], 71), 0)
    kv_pool = draw_kv_pool(jax.random.fold_in(splits[23], 71), 0)
    norm_in = jnp.clip(1.0 + 0.1 * jax.random.normal(splits[5], (D,), jnp.float32), 0.5, 1.5)
    w_query = bell_draw(splits[6], (D, H * HD), D ** -0.5, 0.125, ((1, 4),))
    w_keyval = bell_draw(splits[7], (D, 2 * KVH * HD), D ** -0.5, 0.125)
    q_gain = jnp.clip(jnp.exp(jax.random.uniform(splits[8], (HD,), jnp.float32, math.log(0.1), math.log(0.4))), 0.1, 0.4)
    k_gain = jnp.clip(1.0 + 0.1 * jax.random.normal(splits[9], (HD,), jnp.float32), 0.5, 1.5)
    w_out = bell_draw(splits[10], (H * HD, D), (H * HD) ** -0.5, 0.125, ((0, 4),))
    post_attn_gain = jnp.clip(1.0 + 0.1 * jax.random.normal(splits[11], (D,), jnp.float32), 0.5, 1.5)
    laurel_left = bell_draw(splits[12], (D, RANK), D ** -0.5, 0.125)
    laurel_right = bell_draw(splits[13], (RANK, D), RANK ** -0.5, 0.75)
    laurel_gain = jnp.clip(1.0 + 0.1 * jax.random.normal(splits[14], (D,), jnp.float32), 0.5, 1.5)
    pre_ffn_gain = jnp.clip(1.0 + 0.1 * jax.random.normal(splits[15], (D,), jnp.float32), 0.5, 1.5)
    w_gate = bell_draw(splits[16], (D, FF), D ** -0.5, 0.125, ((1, 4),))
    w_up = bell_draw(splits[17], (D, FF), D ** -0.5, 0.125, ((1, 4),))
    w_down = bell_draw(splits[18], (FF, D), FF ** -0.5, 0.0625, ((0, 4),))
    post_ffn_gain = jnp.clip(1.0 + 0.1 * jax.random.normal(splits[19], (D,), jnp.float32), 0.5, 1.5)
    ple_gate = bell_draw(splits[20], (D, PLE), D ** -0.5, 0.125)
    ple_proj = bell_draw(splits[21], (PLE, D), PLE ** -0.5, 0.375)
    ple_gain = jnp.clip(1.0 + 0.1 * jax.random.normal(splits[22], (D,), jnp.float32), 0.5, 1.5)
    return {"hidden_in": hidden_in, "layer_input": layer_input, "cached_len": cached_len, "page_table": page_table, "kv_pool": kv_pool, "norm_in": norm_in, "w_query": w_query, "w_keyval": w_keyval, "q_gain": q_gain, "k_gain": k_gain, "w_out": w_out, "post_attn_gain": post_attn_gain, "laurel_left": laurel_left, "laurel_right": laurel_right, "laurel_gain": laurel_gain, "pre_ffn_gain": pre_ffn_gain, "w_gate": w_gate, "w_up": w_up, "w_down": w_down, "post_ffn_gain": post_ffn_gain, "ple_gate": ple_gate, "ple_proj": ple_proj, "ple_gain": ple_gain}


EPS = 1e-06
BIG = 1e+30
HALF_ROOT = 1.0 / math.sqrt(2.0)

def norm_rows(values, gain):
    return values * lax.rsqrt(lax.optimization_barrier(jnp.mean(values * values, axis=-1, keepdims=True)) + EPS) * gain

def rotate(values, position):
    half_dim = values.shape[-1] // 2
    freqs = jnp.exp(jnp.arange(half_dim, dtype=jnp.float32) * (-math.log(1000000.0) / half_dim))
    angle = position.astype(jnp.float32)[:, None] * freqs[None, :]
    cosine = jnp.cos(angle)[:, None, :]
    sine = jnp.sin(angle)[:, None, :]
    first = values[..., :half_dim]
    second = values[..., half_dim:]
    return jnp.concatenate([first * cosine - second * sine, second * cosine + first * sine], axis=-1)

def reference(hidden_in, layer_input, cached_len, page_table, kv_pool, norm_in, w_query, w_keyval, q_gain, k_gain, w_out, post_attn_gain, laurel_left, laurel_right, laurel_gain, pre_ffn_gain, w_gate, w_up, w_down, post_ffn_gain, ple_gate, ple_proj, ple_gain):
    grouped = H // KVH
    x_full = hidden_in.astype(jnp.float32)
    normed = norm_rows(x_full, norm_in).astype(jnp.bfloat16)
    offsets = jnp.arange(NEW, dtype=jnp.int32)
    position = (cached_len[:, None] + offsets[None, :]).reshape(-1)
    queries = jnp.dot(normed, w_query, preferred_element_type=jnp.float32).reshape(TOKENS, H, HD)
    queries = rotate(norm_rows(queries, q_gain), position).astype(jnp.bfloat16)
    keyval = jnp.dot(normed, w_keyval, preferred_element_type=jnp.float32).reshape(TOKENS, 2, KVH, HD)
    new_keys = rotate(norm_rows(keyval[:, 0], k_gain), position).astype(jnp.bfloat16)
    new_values = norm_rows(keyval[:, 1], 1.0).astype(jnp.bfloat16)
    causal = (offsets[:, None] >= offsets[None, :])[None, None, :, :]

    def attend(request):
        start = request * NEW
        pages = kv_pool[page_table[request]]
        cache_keys = jnp.transpose(pages[:, 0], (1, 0, 2, 3)).reshape(KVH, SLOTS * PAGE, HD).astype(jnp.float32)
        cache_values = jnp.transpose(pages[:, 1], (1, 0, 2, 3)).reshape(KVH, SLOTS * PAGE, HD).astype(jnp.float32)
        block = lax.dynamic_slice_in_dim(queries, start, NEW, 0).astype(jnp.float32).reshape(NEW, KVH, grouped, HD)
        fresh_keys = lax.dynamic_slice_in_dim(new_keys, start, NEW, 0).astype(jnp.float32)
        fresh_values = lax.dynamic_slice_in_dim(new_values, start, NEW, 0).astype(jnp.float32)
        visible_cache = (jnp.arange(SLOTS * PAGE, dtype=jnp.int32) < cached_len[request])[None, None, None, :]
        score_cache = jnp.where(visible_cache, jnp.einsum('nkgd,kld->kgnl', block, cache_keys), -BIG)
        score_new = jnp.where(causal, jnp.einsum('nkgd,mkd->kgnm', block, fresh_keys), -BIG)
        top = jnp.maximum(lax.optimization_barrier(jnp.max(score_cache, axis=-1, keepdims=True)), lax.optimization_barrier(jnp.max(score_new, axis=-1, keepdims=True)))
        exp_cache = jnp.exp(score_cache - top)
        exp_new = jnp.exp(score_new - top)
        total = lax.optimization_barrier(jnp.sum(exp_cache, axis=-1, keepdims=True)) + lax.optimization_barrier(jnp.sum(exp_new, axis=-1, keepdims=True))
        weight_cache = lax.optimization_barrier((exp_cache / total).astype(jnp.bfloat16)).astype(jnp.float32)
        weight_new = lax.optimization_barrier((exp_new / total).astype(jnp.bfloat16)).astype(jnp.float32)
        mixed = jnp.einsum('kgnl,kld->nkgd', weight_cache, cache_values) + jnp.einsum('kgnm,mkd->nkgd', weight_new, fresh_values)
        return mixed.reshape(NEW, H * HD).astype(jnp.bfloat16)
    attended = lax.map(attend, jnp.arange(REQUESTS, dtype=jnp.int32)).reshape(TOKENS, H * HD)
    projected = jnp.dot(attended, w_out, preferred_element_type=jnp.float32)
    left_part = jnp.dot(normed, laurel_left, preferred_element_type=jnp.float32).astype(jnp.bfloat16)
    laurel_out = normed.astype(jnp.float32) + norm_rows(jnp.dot(left_part, laurel_right, preferred_element_type=jnp.float32), laurel_gain)
    mixed_rows = (x_full + norm_rows(projected, post_attn_gain) + laurel_out) * HALF_ROOT
    ffn_in = norm_rows(mixed_rows, pre_ffn_gain).astype(jnp.bfloat16)

    def feed_forward(block):
        gate_part = jnp.dot(block, w_gate, preferred_element_type=jnp.float32)
        up_part = jnp.dot(block, w_up, preferred_element_type=jnp.float32)
        hidden = (jax.nn.gelu(gate_part, approximate=True) * up_part).astype(jnp.bfloat16)
        return jnp.dot(hidden, w_down, preferred_element_type=jnp.float32)
    down = lax.map(feed_forward, ffn_in.reshape(REQUESTS, NEW, D)).reshape(TOKENS, D)
    settled = mixed_rows + norm_rows(down, post_ffn_gain)
    settled_half = settled.astype(jnp.bfloat16)
    gated = (jax.nn.gelu(jnp.dot(settled_half, ple_gate, preferred_element_type=jnp.float32), approximate=True) * layer_input.astype(jnp.float32)).astype(jnp.bfloat16)
    return (settled + norm_rows(jnp.dot(gated, ple_proj, preferred_element_type=jnp.float32), ple_gain)).astype(jnp.bfloat16)
```

```python
import functools
import math

import jax
import jax.numpy as jnp
from jax import lax
from jax.experimental import pallas as pl
from jax.experimental.pallas import tpu as pltpu
from jax.sharding import PartitionSpec as P

KVH = 2
PROMPT_PAGES = 8
REQ_DEV = 2


EPS = 1e-06
BIG = 1e30
KEY_BLOCK = 1024
SHORTEST = 3584
HALVES = 2
HALF_ROOT = 1.0 / math.sqrt(2.0)


def norm_rows(values, gain):
    return values * lax.rsqrt(jnp.mean(values * values, axis=-1, keepdims=True) + EPS) * gain


def rotate(values, position):
    half_dim = values.shape[-1] // 2
    freqs = jnp.exp(jnp.arange(half_dim, dtype=jnp.float32) * (-math.log(1000000.0) / half_dim))
    angle = position.astype(jnp.float32)[:, None] * freqs[None, :]
    cosine = jnp.cos(angle)[:, None, :]
    sine = jnp.sin(angle)[:, None, :]
    first = values[..., :half_dim]
    second = values[..., half_dim:]
    return jnp.concatenate(
        [first * cosine - second * sine, second * cosine + first * sine], axis=-1
    )


def attend_kernel(
    slots, place, lengths, core, q_ref, off_ref, kn_ref, vn_ref, mine, other, out_ref,
    keys, values, key_sem, value_sem
):
    request = pl.program_id(0)
    first_head = pl.program_id(1) == 0
    page_len = mine.shape[1]
    blocks = slots * page_len // KEY_BLOCK
    per_block = KEY_BLOCK // page_len

    def fetch(key_source, value_source):
        def one(index, carry):
            req = index // slots
            slot = index % slots
            block = slot // per_block
            rows = pl.ds(pl.multiple_of(slot * page_len, page_len), page_len)
            pltpu.make_async_copy(
                key_source.at[place[index]], keys.at[req, rows], key_sem.at[req, block]
            ).start()
            pltpu.make_async_copy(
                value_source.at[place[index]], values.at[req, rows], value_sem.at[req, block]
            ).start()
            return carry

        lax.fori_loop(0, REQ_DEV * slots, one, 0)

    @pl.when(jnp.logical_and(request == 0, first_head))
    def _():
        @pl.when(core[0] == 0)
        def _():
            fetch(mine, other)

        @pl.when(core[0] == 1)
        def _():
            fetch(other, mine)

    query = q_ref[0]
    fresh = kn_ref.shape[1]
    contract_last = (((1,), (1,)), ((), ()))
    score = lax.dot_general(query, kn_ref[0], contract_last, preferred_element_type=jnp.float32)
    visible = off_ref[...] >= lax.broadcasted_iota(jnp.int32, (query.shape[0], fresh), 1)
    score = jnp.where(visible, score, -BIG)
    top = jnp.max(score, axis=-1, keepdims=True)
    weight = jnp.exp(score - top)
    total = jnp.sum(weight, axis=-1, keepdims=True)
    mixed = jnp.dot(weight.astype(jnp.bfloat16), vn_ref[0], preferred_element_type=jnp.float32)
    for block in range(blocks):
        rows = pl.ds(block * KEY_BLOCK, KEY_BLOCK)

        @pl.when(first_head)
        def _():
            part = keys.at[request, rows]
            pltpu.make_async_copy(part, part, key_sem.at[request, block]).wait()
            part = values.at[request, rows]
            pltpu.make_async_copy(part, part, value_sem.at[request, block]).wait()

        score = lax.dot_general(
            query, keys[request, rows, :], contract_last, preferred_element_type=jnp.float32
        )
        if (block + 1) * KEY_BLOCK > SHORTEST:
            at = block * KEY_BLOCK + lax.broadcasted_iota(jnp.int32, score.shape, 1)
            score = jnp.where(at < lengths[request], score, -BIG)
        higher = jnp.maximum(top, jnp.max(score, axis=-1, keepdims=True))
        scale = jnp.exp(top - higher)
        weight = jnp.exp(score - higher)
        total = total * scale + jnp.sum(weight, axis=-1, keepdims=True)
        mixed = mixed * scale + jnp.dot(
            weight.astype(jnp.bfloat16), values[request, rows, :], preferred_element_type=jnp.float32
        )
        top = higher
    out_ref[0] = (mixed / total).astype(out_ref.dtype)


def attend(place, lengths, core, queries, offsets, fresh_keys, fresh_values, mine, other):
    requests, rows, width = queries.shape
    fresh, head_dim = fresh_keys.shape[1:]
    page_len = mine.shape[1]
    slots = place.shape[0] // requests
    heads = width // head_dim
    blocks = slots * page_len // KEY_BLOCK
    pairs = requests * heads * rows * (slots * page_len + fresh)
    return pl.pallas_call(
        functools.partial(attend_kernel, slots),
        out_shape=jax.ShapeDtypeStruct(queries.shape, jnp.bfloat16),
        grid_spec=pltpu.PrefetchScalarGridSpec(
            num_scalar_prefetch=3,
            grid=(requests, heads),
            in_specs=[
                pl.BlockSpec((1, rows, head_dim), lambda r, h, *_: (r, 0, h)),
                pl.BlockSpec((rows, 1), lambda r, h, *_: (0, 0)),
                pl.BlockSpec((1, fresh, head_dim), lambda r, h, *_: (r, 0, 0)),
                pl.BlockSpec((1, fresh, head_dim), lambda r, h, *_: (r, 0, 0)),
                pl.BlockSpec(memory_space=pl.ANY),
                pl.BlockSpec(memory_space=pl.ANY),
            ],
            out_specs=pl.BlockSpec((1, rows, head_dim), lambda r, h, *_: (r, 0, h)),
            scratch_shapes=[
                pltpu.VMEM((requests, slots * page_len, head_dim), jnp.bfloat16),
                pltpu.VMEM((requests, slots * page_len, head_dim), jnp.bfloat16),
                pltpu.SemaphoreType.DMA((requests, blocks)),
                pltpu.SemaphoreType.DMA((requests, blocks)),
            ],
        ),
        compiler_params=pltpu.CompilerParams(vmem_limit_bytes=28 * 1024 * 1024),
        cost_estimate=pl.CostEstimate(
            flops=4 * pairs * head_dim, bytes_accessed=2 * mine.size * 2, transcendentals=pairs
        ),
    )(place, lengths, core, queries, offsets, fresh_keys, fresh_values, mine, other)


def swap_cores(values, tp_count):
    return lax.ppermute(values, "tensor", [(t, t ^ 1) for t in range(tp_count)])


def shift_chips(values, tp_count, step):
    return lax.ppermute(values, "tensor", [(t, (t + 2 * step) % tp_count) for t in range(tp_count)])


def spread_rows(block, tp_count):
    pieces = [block, swap_cores(block, tp_count)]
    for step in range(1, tp_count // 2):
        came = shift_chips(block, tp_count, step)
        pieces += [came, swap_cores(came, tp_count)]
    return jnp.concatenate(pieces, axis=0)


def collect_rows(partial, tp_count):
    chips = tp_count // 2
    partial = partial.reshape(chips, 2, -1, partial.shape[-1])
    came = swap_cores(partial[:, 1].astype(jnp.bfloat16), tp_count)
    joined = partial[:, 0].astype(jnp.float32) + came.astype(jnp.float32)
    total = joined[0]
    for step in range(1, chips):
        came = shift_chips(joined[step].astype(jnp.bfloat16), tp_count, -step)
        total = total + came.astype(jnp.float32)
    return total


def geglu(block, w_gate, w_up):
    gate_part = jnp.dot(block, w_gate, preferred_element_type=jnp.float32)
    up_part = jnp.dot(block, w_up, preferred_element_type=jnp.float32)
    return (jax.nn.gelu(gate_part, approximate=True) * up_part).astype(jnp.bfloat16)


def per_device(
    hidden_in,
    layer_input,
    cached_len,
    page_table,
    kv_pool,
    norm_in,
    w_query,
    w_keyval,
    q_gain,
    k_gain,
    w_out,
    post_attn_gain,
    laurel_left,
    laurel_right,
    laurel_gain,
    pre_ffn_gain,
    w_gate,
    w_up,
    w_down,
    post_ffn_gain,
    ple_gate,
    ple_proj,
    ple_gain,
):
    dp_count = lax.axis_size("dp")
    tp_count = lax.axis_size("tensor")
    devices = dp_count * tp_count
    dp_at = lax.axis_index("dp")
    tp_at = lax.axis_index("tensor")
    chips = tp_count // 2
    chip_at = tp_at // 2
    core_at = tp_at % 2
    own_rows = hidden_in.shape[0]
    half_rows = own_rows // HALVES
    head_dim = q_gain.shape[0]
    local_heads = w_query.shape[1] // head_dim
    sharing = tp_count // KVH
    kv_head = tp_at // sharing
    slot_count = page_table.shape[1]
    page_len = kv_pool.shape[3]
    pool_dev = kv_pool.shape[0]
    needed = PROMPT_PAGES + REQ_DEV * (slot_count - PROMPT_PAGES)
    capacity = (needed + devices - 1) // devices
    page_count = (cached_len + page_len - 1) // page_len
    used_slots = jnp.arange(slot_count, dtype=jnp.int32)[None, :] < page_count[:, None]
    group_used = used_slots.reshape(dp_count, REQ_DEV * slot_count)
    group_table = page_table.reshape(dp_count, REQ_DEV * slot_count)
    own_flat = dp_at * tp_count + tp_at
    own_ids = own_flat * pool_dev + jnp.arange(pool_dev, dtype=jnp.int32)
    wanted = jnp.any(
        group_used[:, :, None] & (group_table[:, :, None] == own_ids[None, None, :]), axis=1
    )
    wanted_rank = jnp.cumsum(wanted.astype(jnp.int32), axis=1) - 1
    slot_ids = jnp.arange(capacity, dtype=jnp.int32)
    selector = (wanted[:, None, :] & (wanted_rank[:, None, :] == slot_ids[None, :, None])).astype(
        jnp.bfloat16
    )
    picked = jnp.einsum(
        "dcl,lkhpe->dhkcpe", selector, kv_pool, preferred_element_type=jnp.float32
    ).astype(jnp.bfloat16)
    outgoing = jnp.broadcast_to(
        picked[:, :, None],
        (dp_count, KVH, sharing // 2, 2, capacity, page_len, head_dim),
    ).reshape(devices, capacity, page_len, head_dim)
    arrived = lax.all_to_all(outgoing, ("dp", "tensor"), split_axis=0, concat_axis=0, tiled=True)
    mine = arrived.reshape(devices * capacity, page_len, head_dim)
    other = swap_cores(mine, tp_count)
    own_used = lax.dynamic_index_in_dim(group_used, dp_at, 0, keepdims=False)
    own_table = lax.dynamic_index_in_dim(group_table, dp_at, 0, keepdims=False)
    every_page = jnp.arange(devices * pool_dev, dtype=jnp.int32)
    present = jnp.any(own_used[None, :] & (own_table[None, :] == every_page[:, None]), axis=1)
    present_rank = (
        jnp.cumsum(present.reshape(devices, pool_dev).astype(jnp.int32), axis=1) - 1
    ).reshape(-1)
    place = jnp.where(own_used, own_table // pool_dev * capacity + present_rank[own_table], 0)
    own_lengths = lax.dynamic_slice_in_dim(cached_len, dp_at * REQ_DEV, REQ_DEV, 0)
    gathered = lax.all_gather(hidden_in, "tensor", axis=0, tiled=True)
    token_count = gathered.shape[0]
    new_count = token_count // REQ_DEV
    normed = norm_rows(gathered.astype(jnp.float32), norm_in).astype(jnp.bfloat16)
    offsets = jnp.arange(new_count, dtype=jnp.int32)
    position = (own_lengths[:, None] + offsets[None, :]).reshape(-1)
    queries = jnp.dot(normed, w_query, preferred_element_type=jnp.float32).reshape(
        token_count, local_heads, head_dim
    )
    queries = rotate(norm_rows(queries, q_gain), position).astype(jnp.bfloat16)
    key_weight = lax.dynamic_slice_in_dim(w_keyval, kv_head * head_dim, head_dim, 1)
    value_weight = lax.dynamic_slice_in_dim(w_keyval, (KVH + kv_head) * head_dim, head_dim, 1)
    fresh_keys = norm_rows(jnp.dot(normed, key_weight, preferred_element_type=jnp.float32), k_gain)
    fresh_keys = rotate(fresh_keys[:, None, :], position)[:, 0].astype(jnp.bfloat16)
    fresh_values = norm_rows(
        jnp.dot(normed, value_weight, preferred_element_type=jnp.float32), 1.0
    ).astype(jnp.bfloat16)
    fresh_keys = fresh_keys.reshape(REQ_DEV, new_count, head_dim)
    fresh_values = fresh_values.reshape(REQ_DEV, new_count, head_dim)
    by_half = (REQ_DEV, tp_count // REQ_DEV, HALVES, half_rows, local_heads * head_dim)
    queries = queries.reshape(by_half)
    offsets = offsets.reshape(by_half[1:4])

    own_x = hidden_in.astype(jnp.float32)
    own_normed = norm_rows(own_x, norm_in).astype(jnp.bfloat16)
    left_part = jnp.dot(own_normed, laurel_left, preferred_element_type=jnp.float32).astype(
        jnp.bfloat16
    )
    laurel_out = own_normed.astype(jnp.float32) + norm_rows(
        jnp.dot(left_part, laurel_right, preferred_element_type=jnp.float32), laurel_gain
    )
    beside = own_x + laurel_out

    owners = [
        (chip_at - step + chips) % chips * 2 + (core_at if same == 0 else 1 - core_at)
        for step in range(chips)
        for same in range(2)
    ]
    core_flag = core_at.reshape(1).astype(jnp.int32)
    projected = []
    for half in range(HALVES):
        attended = attend(
            place,
            own_lengths,
            core_flag,
            queries[:, :, half].reshape(REQ_DEV, new_count // HALVES, -1),
            offsets[:, half].reshape(-1, 1),
            fresh_keys,
            fresh_values,
            mine,
            other,
        ).reshape(tp_count, half_rows, -1)
        attended = jnp.concatenate(
            [lax.dynamic_index_in_dim(attended, owner, 0, keepdims=False) for owner in owners]
        )
        projected.append(
            collect_rows(jnp.dot(attended, w_out, preferred_element_type=jnp.float32), tp_count)
        )
    mixed_halves, entering = [], []
    for half in range(HALVES):
        rows = slice(half * half_rows, (half + 1) * half_rows)
        mixed_rows = (beside[rows] + norm_rows(projected[half], post_attn_gain)) * HALF_ROOT
        mixed_halves.append(mixed_rows)
        ffn_in = norm_rows(mixed_rows, pre_ffn_gain).astype(jnp.bfloat16)
        entering.append(spread_rows(ffn_in, tp_count))
    results = []
    for half in range(HALVES):
        rows = slice(half * half_rows, (half + 1) * half_rows)
        hidden = geglu(entering[half], w_gate, w_up)
        down = collect_rows(
            jnp.dot(hidden, w_down, preferred_element_type=jnp.float32).astype(jnp.bfloat16),
            tp_count,
        )
        settled = mixed_halves[half] + norm_rows(down, post_ffn_gain)
        settled_half = settled.astype(jnp.bfloat16)
        gated = jax.nn.gelu(
            jnp.dot(settled_half, ple_gate, preferred_element_type=jnp.float32), approximate=True
        )
        gated = (gated * layer_input[rows].astype(jnp.float32)).astype(jnp.bfloat16)
        results.append(
            (
                settled
                + norm_rows(
                    jnp.dot(gated, ple_proj, preferred_element_type=jnp.float32), ple_gain
                )
            ).astype(jnp.bfloat16)
        )
    return jnp.concatenate(results, axis=0)


def solution(mesh):
    placed = (
        P(("dp", "tensor"), None),
        P(("dp", "tensor"), None),
        P(),
        P(),
        P(("dp", "tensor"), None, None, None, None),
        P(),
        P(None, "tensor"),
        P(),
        P(),
        P(),
        P("tensor", None),
        P(),
        P(),
        P(),
        P(),
        P(),
        P(None, "tensor"),
        P(None, "tensor"),
        P("tensor", None),
        P(),
        P(),
        P(),
        P(),
    )
    return jax.shard_map(
        per_device, mesh=mesh, in_specs=placed, out_specs=P(("dp", "tensor"), None), check_vma=False
    )
```

```python
import functools
import math

import jax
import jax.numpy as jnp
from jax import lax
from jax.experimental import pallas as pl
from jax.experimental.pallas import tpu as pltpu
from jax.sharding import PartitionSpec as P

KVH = 2
PROMPT_PAGES = 8
REQ_DEV = 2


EPS = 1e-06
BIG = 1e30
KEY_BLOCK = 1024
SHORTEST = 3584
HALVES = 2
HALF_ROOT = 1.0 / math.sqrt(2.0)


def norm_rows(values, gain):
    return values * lax.rsqrt(jnp.mean(values * values, axis=-1, keepdims=True) + EPS) * gain


def rotate(values, position):
    half_dim = values.shape[-1] // 2
    freqs = jnp.exp(jnp.arange(half_dim, dtype=jnp.float32) * (-math.log(1000000.0) / half_dim))
    angle = position.astype(jnp.float32)[:, None] * freqs[None, :]
    cosine = jnp.cos(angle)[:, None, :]
    sine = jnp.sin(angle)[:, None, :]
    first = values[..., :half_dim]
    second = values[..., half_dim:]
    return jnp.concatenate(
        [first * cosine - second * sine, second * cosine + first * sine], axis=-1
    )


def attend_kernel(
    slots, place, lengths, core, q_ref, off_ref, kn_ref, vn_ref, mine, other, out_ref,
    keys, values, key_sem, value_sem
):
    request = pl.program_id(0)
    first_head = pl.program_id(1) == 0
    page_len = mine.shape[1]
    blocks = slots * page_len // KEY_BLOCK
    per_block = KEY_BLOCK // page_len

    def fetch(key_source, value_source):
        def one(index, carry):
            req = index // slots
            slot = index % slots
            block = slot // per_block
            rows = pl.ds(pl.multiple_of(slot * page_len, page_len), page_len)
            pltpu.make_async_copy(
                key_source.at[place[index]], keys.at[req, rows], key_sem.at[req, block]
            ).start()
            pltpu.make_async_copy(
                value_source.at[place[index]], values.at[req, rows], value_sem.at[req, block]
            ).start()
            return carry

        lax.fori_loop(0, REQ_DEV * slots, one, 0)

    @pl.when(jnp.logical_and(request == 0, first_head))
    def _():
        @pl.when(core[0] == 0)
        def _():
            fetch(mine, other)

        @pl.when(core[0] == 1)
        def _():
            fetch(other, mine)

    @pl.when(first_head)
    def _():
        for block in range(blocks):
            rows = pl.ds(block * KEY_BLOCK, KEY_BLOCK)
            part = keys.at[request, rows]
            pltpu.make_async_copy(part, part, key_sem.at[request, block]).wait()
            part = values.at[request, rows]
            pltpu.make_async_copy(part, part, value_sem.at[request, block]).wait()

    query = q_ref[0]
    fresh = kn_ref.shape[1]

    def match(block_keys):
        return lax.dot_general(
            query, block_keys, (((1,), (1,)), ((), ())), preferred_element_type=jnp.float32
        )

    def cached(block):
        score = match(keys[request, pl.ds(block * KEY_BLOCK, KEY_BLOCK), :])
        if (block + 1) * KEY_BLOCK > SHORTEST:
            at = block * KEY_BLOCK + lax.broadcasted_iota(jnp.int32, score.shape, 1)
            score = jnp.where(at < lengths[request], score, -BIG)
        return score

    score = match(kn_ref[0])
    ahead = cached(0)
    visible = off_ref[...] >= lax.broadcasted_iota(jnp.int32, (query.shape[0], fresh), 1)
    score = jnp.where(visible, score, -BIG)
    top = jnp.max(score, axis=-1, keepdims=True)
    weight = jnp.exp(score - top)
    total = jnp.sum(weight, axis=-1, keepdims=True)
    mixed = jnp.dot(weight.astype(jnp.bfloat16), vn_ref[0], preferred_element_type=jnp.float32)
    for block in range(blocks):
        score = ahead
        if block + 1 < blocks:
            ahead = cached(block + 1)
        higher = jnp.maximum(top, jnp.max(score, axis=-1, keepdims=True))
        scale = jnp.exp(top - higher)
        weight = jnp.exp(score - higher)
        total = total * scale + jnp.sum(weight, axis=-1, keepdims=True)
        mixed = mixed * scale + jnp.dot(
            weight.astype(jnp.bfloat16),
            values[request, pl.ds(block * KEY_BLOCK, KEY_BLOCK), :],
            preferred_element_type=jnp.float32,
        )
        top = higher
    out_ref[0] = (mixed / total).astype(out_ref.dtype)


def attend(place, lengths, core, queries, offsets, fresh_keys, fresh_values, mine, other):
    requests, rows, width = queries.shape
    fresh, head_dim = fresh_keys.shape[1:]
    page_len = mine.shape[1]
    slots = place.shape[0] // requests
    heads = width // head_dim
    blocks = slots * page_len // KEY_BLOCK
    pairs = requests * heads * rows * (slots * page_len + fresh)
    return pl.pallas_call(
        functools.partial(attend_kernel, slots),
        out_shape=jax.ShapeDtypeStruct(queries.shape, jnp.bfloat16),
        grid_spec=pltpu.PrefetchScalarGridSpec(
            num_scalar_prefetch=3,
            grid=(requests, heads),
            in_specs=[
                pl.BlockSpec((1, rows, head_dim), lambda r, h, *_: (r, 0, h)),
                pl.BlockSpec((rows, 1), lambda r, h, *_: (0, 0)),
                pl.BlockSpec((1, fresh, head_dim), lambda r, h, *_: (r, 0, 0)),
                pl.BlockSpec((1, fresh, head_dim), lambda r, h, *_: (r, 0, 0)),
                pl.BlockSpec(memory_space=pl.ANY),
                pl.BlockSpec(memory_space=pl.ANY),
            ],
            out_specs=pl.BlockSpec((1, rows, head_dim), lambda r, h, *_: (r, 0, h)),
            scratch_shapes=[
                pltpu.VMEM((requests, slots * page_len, head_dim), jnp.bfloat16),
                pltpu.VMEM((requests, slots * page_len, head_dim), jnp.bfloat16),
                pltpu.SemaphoreType.DMA((requests, blocks)),
                pltpu.SemaphoreType.DMA((requests, blocks)),
            ],
        ),
        compiler_params=pltpu.CompilerParams(vmem_limit_bytes=28 * 1024 * 1024),
        cost_estimate=pl.CostEstimate(
            flops=4 * pairs * head_dim, bytes_accessed=2 * mine.size * 2, transcendentals=pairs
        ),
    )(place, lengths, core, queries, offsets, fresh_keys, fresh_values, mine, other)


def swap_cores(values, tp_count):
    return lax.ppermute(values, "tensor", [(t, t ^ 1) for t in range(tp_count)])


def shift_chips(values, tp_count, step):
    return lax.ppermute(values, "tensor", [(t, (t + 2 * step) % tp_count) for t in range(tp_count)])


def spread_rows(block, tp_count):
    pieces = [block, swap_cores(block, tp_count)]
    for step in range(1, tp_count // 2):
        came = shift_chips(block, tp_count, step)
        pieces += [came, swap_cores(came, tp_count)]
    return pieces


def join_cores(partial, tp_count):
    came = swap_cores(partial[:, 1].astype(jnp.bfloat16), tp_count)
    return partial[:, 0].astype(jnp.float32) + came.astype(jnp.float32)


def join_chips(joined, total, tp_count):
    for step in range(1, joined.shape[0] + 1):
        came = shift_chips(joined[step - 1].astype(jnp.bfloat16), tp_count, -step)
        total = total + came.astype(jnp.float32)
    return total


def ffn_kernel(x_ref, gate_ref, up_ref, down_ref, out_ref, total):
    step = pl.program_id(0)
    block = x_ref[...]
    gate_part = jnp.dot(block, gate_ref[...], preferred_element_type=jnp.float32)
    up_part = jnp.dot(block, up_ref[...], preferred_element_type=jnp.float32)
    hidden = (jax.nn.gelu(gate_part, approximate=True) * up_part).astype(jnp.bfloat16)
    part = jnp.dot(hidden, down_ref[...], preferred_element_type=jnp.float32)

    @pl.when(step == 0)
    def _():
        total[...] = part

    @pl.when(step > 0)
    def _():
        total[...] += part

    @pl.when(step == pl.num_programs(0) - 1)
    def _():
        out_ref[...] = total[...].astype(out_ref.dtype)


def feed_forward(block, w_gate, w_up, w_down):
    rows, width = block.shape
    units = w_gate.shape[1]
    tile = min(512, units)
    return pl.pallas_call(
        ffn_kernel,
        out_shape=jax.ShapeDtypeStruct(block.shape, jnp.bfloat16),
        grid=(units // tile,),
        in_specs=[
            pl.BlockSpec((rows, width), lambda i: (0, 0)),
            pl.BlockSpec((width, tile), lambda i: (0, i)),
            pl.BlockSpec((width, tile), lambda i: (0, i)),
            pl.BlockSpec((tile, width), lambda i: (i, 0)),
        ],
        out_specs=pl.BlockSpec((rows, width), lambda i: (0, 0)),
        scratch_shapes=[pltpu.VMEM((rows, width), jnp.float32)],
        compiler_params=pltpu.CompilerParams(vmem_limit_bytes=40 * 1024 * 1024),
        cost_estimate=pl.CostEstimate(
            flops=6 * rows * width * units,
            bytes_accessed=6 * width * units,
            transcendentals=rows * units,
        ),
    )(block, w_gate, w_up, w_down)


def per_device(
    hidden_in,
    layer_input,
    cached_len,
    page_table,
    kv_pool,
    norm_in,
    w_query,
    w_keyval,
    q_gain,
    k_gain,
    w_out,
    post_attn_gain,
    laurel_left,
    laurel_right,
    laurel_gain,
    pre_ffn_gain,
    w_gate,
    w_up,
    w_down,
    post_ffn_gain,
    ple_gate,
    ple_proj,
    ple_gain,
):
    dp_count = lax.axis_size("dp")
    tp_count = lax.axis_size("tensor")
    devices = dp_count * tp_count
    dp_at = lax.axis_index("dp")
    tp_at = lax.axis_index("tensor")
    chips = tp_count // 2
    chip_at = tp_at // 2
    core_at = tp_at % 2
    own_rows = hidden_in.shape[0]
    half_rows = own_rows // HALVES
    head_dim = q_gain.shape[0]
    local_heads = w_query.shape[1] // head_dim
    sharing = tp_count // KVH
    kv_head = tp_at // sharing
    slot_count = page_table.shape[1]
    page_len = kv_pool.shape[3]
    pool_dev = kv_pool.shape[0]
    needed = PROMPT_PAGES + REQ_DEV * (slot_count - PROMPT_PAGES)
    capacity = (needed + devices - 1) // devices
    page_count = (cached_len + page_len - 1) // page_len
    used_slots = jnp.arange(slot_count, dtype=jnp.int32)[None, :] < page_count[:, None]
    group_used = used_slots.reshape(dp_count, REQ_DEV * slot_count)
    group_table = page_table.reshape(dp_count, REQ_DEV * slot_count)
    own_flat = dp_at * tp_count + tp_at
    own_ids = own_flat * pool_dev + jnp.arange(pool_dev, dtype=jnp.int32)
    wanted = jnp.any(
        group_used[:, :, None] & (group_table[:, :, None] == own_ids[None, None, :]), axis=1
    )
    wanted_rank = jnp.cumsum(wanted.astype(jnp.int32), axis=1) - 1
    slot_ids = jnp.arange(capacity, dtype=jnp.int32)
    selector = (wanted[:, None, :] & (wanted_rank[:, None, :] == slot_ids[None, :, None])).astype(
        jnp.bfloat16
    )
    picked = jnp.einsum(
        "dcl,lkhpe->dhkcpe", selector, kv_pool, preferred_element_type=jnp.float32
    ).astype(jnp.bfloat16)
    outgoing = jnp.broadcast_to(
        picked[:, :, None],
        (dp_count, KVH, sharing // 2, 2, capacity, page_len, head_dim),
    ).reshape(devices, capacity, page_len, head_dim)
    arrived = lax.all_to_all(outgoing, ("dp", "tensor"), split_axis=0, concat_axis=0, tiled=True)
    own_used = lax.dynamic_index_in_dim(group_used, dp_at, 0, keepdims=False)
    own_table = lax.dynamic_index_in_dim(group_table, dp_at, 0, keepdims=False)
    every_page = jnp.arange(devices * pool_dev, dtype=jnp.int32)
    present = jnp.any(own_used[None, :] & (own_table[None, :] == every_page[:, None]), axis=1)
    present_rank = (
        jnp.cumsum(present.reshape(devices, pool_dev).astype(jnp.int32), axis=1) - 1
    ).reshape(-1)
    place = jnp.where(own_used, own_table // pool_dev * capacity + present_rank[own_table], 0)
    own_lengths = lax.dynamic_slice_in_dim(cached_len, dp_at * REQ_DEV, REQ_DEV, 0)
    near = jnp.stack(spread_rows(hidden_in, tp_count))
    gathered = jnp.concatenate(
        [
            lax.dynamic_index_in_dim(
                near, (chip_at - t // 2 + chips) % chips * 2 + (core_at + t) % 2, 0, keepdims=False
            )
            for t in range(tp_count)
        ]
    )
    token_count = gathered.shape[0]
    new_count = token_count // REQ_DEV
    normed = norm_rows(gathered.astype(jnp.float32), norm_in).astype(jnp.bfloat16)
    offsets = jnp.arange(new_count, dtype=jnp.int32)
    position = (own_lengths[:, None] + offsets[None, :]).reshape(-1)
    queries = jnp.dot(normed, w_query, preferred_element_type=jnp.float32).reshape(
        token_count, local_heads, head_dim
    )
    queries = rotate(norm_rows(queries, q_gain), position).astype(jnp.bfloat16)
    key_weight = lax.dynamic_slice_in_dim(w_keyval, kv_head * head_dim, head_dim, 1)
    value_weight = lax.dynamic_slice_in_dim(w_keyval, (KVH + kv_head) * head_dim, head_dim, 1)
    fresh_keys = norm_rows(jnp.dot(normed, key_weight, preferred_element_type=jnp.float32), k_gain)
    fresh_keys = rotate(fresh_keys[:, None, :], position)[:, 0].astype(jnp.bfloat16)
    fresh_values = norm_rows(
        jnp.dot(normed, value_weight, preferred_element_type=jnp.float32), 1.0
    ).astype(jnp.bfloat16)
    fresh_keys = fresh_keys.reshape(REQ_DEV, new_count, head_dim)
    fresh_values = fresh_values.reshape(REQ_DEV, new_count, head_dim)
    by_half = (REQ_DEV, tp_count // REQ_DEV, HALVES, half_rows, local_heads * head_dim)
    arrived, queries, fresh_keys, fresh_values = lax.optimization_barrier(
        (arrived, queries, fresh_keys, fresh_values)
    )
    mine = arrived.reshape(devices * capacity, page_len, head_dim)
    other = swap_cores(mine, tp_count)
    queries = queries.reshape(by_half)
    offsets = offsets.reshape(by_half[1:4])

    own_x = hidden_in.astype(jnp.float32)
    own_normed = norm_rows(own_x, norm_in).astype(jnp.bfloat16)
    left_part = jnp.dot(own_normed, laurel_left, preferred_element_type=jnp.float32).astype(
        jnp.bfloat16
    )
    laurel_out = own_normed.astype(jnp.float32) + norm_rows(
        jnp.dot(left_part, laurel_right, preferred_element_type=jnp.float32), laurel_gain
    )
    beside = own_x + laurel_out

    owners = [
        (chip_at - step + chips) % chips * 2 + (core_at if same == 0 else 1 - core_at)
        for step in range(chips)
        for same in range(2)
    ]
    core_flag = core_at.reshape(1).astype(jnp.int32)
    width = hidden_in.shape[1]
    joined = []
    for half in range(HALVES):
        half_queries = queries[:, :, half].reshape(REQ_DEV, new_count // HALVES, -1)
        if half:
            half_queries, joined[-1] = lax.optimization_barrier((half_queries, joined[-1]))
        attended = attend(
            place,
            own_lengths,
            core_flag,
            half_queries,
            offsets[:, half].reshape(-1, 1),
            fresh_keys,
            fresh_values,
            mine,
            other,
        ).reshape(tp_count, half_rows, -1)
        attended = jnp.concatenate(
            [lax.dynamic_index_in_dim(attended, owner, 0, keepdims=False) for owner in owners]
        )
        partial = jnp.dot(attended, w_out, preferred_element_type=jnp.float32)
        joined.append(join_cores(partial.reshape(chips, 2, half_rows, width), tp_count))
    mixed_halves, entering = [], []
    for half in range(HALVES):
        rows = slice(half * half_rows, (half + 1) * half_rows)
        projected = join_chips(joined[half][1:], joined[half][0], tp_count)
        mixed_rows = (beside[rows] + norm_rows(projected, post_attn_gain)) * HALF_ROOT
        mixed_halves.append(mixed_rows)
        ffn_in = norm_rows(mixed_rows, pre_ffn_gain).astype(jnp.bfloat16)
        entering.append(spread_rows(ffn_in, tp_count))
    near_down, far_down = [], []
    last = None
    for pick, kept in ((slice(0, 2), near_down), (slice(2, None), far_down)):
        for half in range(HALVES):
            block = jnp.concatenate(entering[half][pick])
            if last is not None:
                block, last[-1] = lax.optimization_barrier((block, last[-1]))
            kept.append(feed_forward(block, w_gate, w_up, w_down))
            last = kept
    results = []
    for half in range(HALVES):
        rows = slice(half * half_rows, (half + 1) * half_rows)
        near_sum = join_cores(near_down[half].reshape(1, 2, half_rows, width), tp_count)[0]
        far_sum = join_cores(far_down[half].reshape(chips - 1, 2, half_rows, width), tp_count)
        down = join_chips(far_sum, near_sum, tp_count)
        settled = mixed_halves[half] + norm_rows(down, post_ffn_gain)
        settled_half = settled.astype(jnp.bfloat16)
        gated = jax.nn.gelu(
            jnp.dot(settled_half, ple_gate, preferred_element_type=jnp.float32), approximate=True
        )
        gated = (gated * layer_input[rows].astype(jnp.float32)).astype(jnp.bfloat16)
        results.append(
            (
                settled
                + norm_rows(
                    jnp.dot(gated, ple_proj, preferred_element_type=jnp.float32), ple_gain
                )
            ).astype(jnp.bfloat16)
        )
    return jnp.concatenate(results, axis=0)


def solution(mesh):
    placed = (
        P(("dp", "tensor"), None),
        P(("dp", "tensor"), None),
        P(),
        P(),
        P(("dp", "tensor"), None, None, None, None),
        P(),
        P(None, "tensor"),
        P(),
        P(),
        P(),
        P("tensor", None),
        P(),
        P(),
        P(),
        P(),
        P(),
        P(None, "tensor"),
        P(None, "tensor"),
        P("tensor", None),
        P(),
        P(),
        P(),
        P(),
    )
    return jax.shard_map(
        per_device, mesh=mesh, in_specs=placed, out_specs=P(("dp", "tensor"), None), check_vma=False
    )
```

```python
import functools
import math

import jax
import jax.numpy as jnp
from jax import lax
from jax.experimental import pallas as pl
from jax.experimental.pallas import tpu as pltpu
from jax.sharding import PartitionSpec as P

KVH = 2
PROMPT_PAGES = 8
REQ_DEV = 2


EPS = 1e-06
BIG = 1e30
KEY_BLOCK = 1024
SHORTEST = 3584
HALVES = 2
HALF_ROOT = 1.0 / math.sqrt(2.0)


def norm_rows(values, gain):
    return values * lax.rsqrt(jnp.mean(values * values, axis=-1, keepdims=True) + EPS) * gain


def rotate(values, position):
    half_dim = values.shape[-1] // 2
    freqs = jnp.exp(jnp.arange(half_dim, dtype=jnp.float32) * (-math.log(1000000.0) / half_dim))
    angle = position.astype(jnp.float32)[:, None] * freqs[None, :]
    cosine = jnp.cos(angle)[:, None, :]
    sine = jnp.sin(angle)[:, None, :]
    first = values[..., :half_dim]
    second = values[..., half_dim:]
    return jnp.concatenate(
        [first * cosine - second * sine, second * cosine + first * sine], axis=-1
    )


def attend_kernel(
    slots, place, lengths, core, q_ref, off_ref, kn_ref, vn_ref, mine, other, out_ref,
    keys, values, key_sem, value_sem
):
    request = pl.program_id(0)
    first_head = pl.program_id(1) == 0
    page_len = mine.shape[1]
    blocks = slots * page_len // KEY_BLOCK
    per_block = KEY_BLOCK // page_len

    def fetch(key_source, value_source):
        def one(index, carry):
            req = index // slots
            slot = index % slots
            block = slot // per_block
            rows = pl.ds(pl.multiple_of(slot * page_len, page_len), page_len)
            pltpu.make_async_copy(
                key_source.at[place[index]], keys.at[req, rows], key_sem.at[req, block]
            ).start()
            pltpu.make_async_copy(
                value_source.at[place[index]], values.at[req, rows], value_sem.at[req, block]
            ).start()
            return carry

        lax.fori_loop(0, REQ_DEV * slots, one, 0)

    @pl.when(jnp.logical_and(request == 0, first_head))
    def _():
        @pl.when(core[0] == 0)
        def _():
            fetch(mine, other)

        @pl.when(core[0] == 1)
        def _():
            fetch(other, mine)

    @pl.when(first_head)
    def _():
        for block in range(blocks):
            rows = pl.ds(block * KEY_BLOCK, KEY_BLOCK)
            part = keys.at[request, rows]
            pltpu.make_async_copy(part, part, key_sem.at[request, block]).wait()
            part = values.at[request, rows]
            pltpu.make_async_copy(part, part, value_sem.at[request, block]).wait()

    query = q_ref[0]
    fresh = kn_ref.shape[1]

    def match(block_keys):
        return lax.dot_general(
            query, block_keys, (((1,), (1,)), ((), ())), preferred_element_type=jnp.float32
        )

    def cached(block):
        score = match(keys[request, pl.ds(block * KEY_BLOCK, KEY_BLOCK), :])
        if (block + 1) * KEY_BLOCK > SHORTEST:
            at = block * KEY_BLOCK + lax.broadcasted_iota(jnp.int32, score.shape, 1)
            score = jnp.where(at < lengths[request], score, -BIG)
        return score

    score = match(kn_ref[0])
    ahead = cached(0)
    visible = off_ref[...] >= lax.broadcasted_iota(jnp.int32, (query.shape[0], fresh), 1)
    score = jnp.where(visible, score, -BIG)
    top = jnp.max(score, axis=-1, keepdims=True)
    weight = jnp.exp(score - top)
    total = jnp.sum(weight, axis=-1, keepdims=True)
    mixed = jnp.dot(weight.astype(jnp.bfloat16), vn_ref[0], preferred_element_type=jnp.float32)
    for block in range(blocks):
        score = ahead
        if block + 1 < blocks:
            ahead = cached(block + 1)
        higher = jnp.maximum(top, jnp.max(score, axis=-1, keepdims=True))
        scale = jnp.exp(top - higher)
        weight = jnp.exp(score - higher)
        total = total * scale + jnp.sum(weight, axis=-1, keepdims=True)
        mixed = mixed * scale + jnp.dot(
            weight.astype(jnp.bfloat16),
            values[request, pl.ds(block * KEY_BLOCK, KEY_BLOCK), :],
            preferred_element_type=jnp.float32,
        )
        top = higher
    out_ref[0] = (mixed / total).astype(out_ref.dtype)


def attend(place, lengths, core, queries, offsets, fresh_keys, fresh_values, mine, other):
    requests, rows, width = queries.shape
    fresh, head_dim = fresh_keys.shape[1:]
    page_len = mine.shape[1]
    slots = place.shape[0] // requests
    heads = width // head_dim
    blocks = slots * page_len // KEY_BLOCK
    pairs = requests * heads * rows * (slots * page_len + fresh)
    return pl.pallas_call(
        functools.partial(attend_kernel, slots),
        out_shape=jax.ShapeDtypeStruct(queries.shape, jnp.bfloat16),
        grid_spec=pltpu.PrefetchScalarGridSpec(
            num_scalar_prefetch=3,
            grid=(requests, heads),
            in_specs=[
                pl.BlockSpec((1, rows, head_dim), lambda r, h, *_: (r, 0, h)),
                pl.BlockSpec((rows, 1), lambda r, h, *_: (0, 0)),
                pl.BlockSpec((1, fresh, head_dim), lambda r, h, *_: (r, 0, 0)),
                pl.BlockSpec((1, fresh, head_dim), lambda r, h, *_: (r, 0, 0)),
                pl.BlockSpec(memory_space=pl.ANY),
                pl.BlockSpec(memory_space=pl.ANY),
            ],
            out_specs=pl.BlockSpec((1, rows, head_dim), lambda r, h, *_: (r, 0, h)),
            scratch_shapes=[
                pltpu.VMEM((requests, slots * page_len, head_dim), jnp.bfloat16),
                pltpu.VMEM((requests, slots * page_len, head_dim), jnp.bfloat16),
                pltpu.SemaphoreType.DMA((requests, blocks)),
                pltpu.SemaphoreType.DMA((requests, blocks)),
            ],
        ),
        compiler_params=pltpu.CompilerParams(vmem_limit_bytes=28 * 1024 * 1024),
        cost_estimate=pl.CostEstimate(
            flops=4 * pairs * head_dim, bytes_accessed=2 * mine.size * 2, transcendentals=pairs
        ),
    )(place, lengths, core, queries, offsets, fresh_keys, fresh_values, mine, other)


def swap_cores(values, tp_count):
    return lax.ppermute(values, "tensor", [(t, t ^ 1) for t in range(tp_count)])


def shift_chips(values, tp_count, step):
    return lax.ppermute(values, "tensor", [(t, (t + 2 * step) % tp_count) for t in range(tp_count)])


def spread_rows(block, tp_count):
    pieces = [block, swap_cores(block, tp_count)]
    for step in range(1, tp_count // 2):
        came = shift_chips(block, tp_count, step)
        pieces += [came, swap_cores(came, tp_count)]
    return pieces


def join_cores(partial, tp_count):
    came = swap_cores(partial[:, 1].astype(jnp.bfloat16), tp_count)
    joined = partial[:, 0].astype(jnp.float32) + came.astype(jnp.float32)
    return joined, joined.astype(jnp.bfloat16)


def send_chips(leaving, tp_count):
    return [
        shift_chips(leaving[step - 1], tp_count, -step) for step in range(1, leaving.shape[0] + 1)
    ]


def add_all(total, pieces):
    for piece in pieces:
        total = total + piece.astype(jnp.float32)
    return total


def ffn_kernel(x_ref, gate_ref, up_ref, down_ref, out_ref, total):
    step = pl.program_id(0)
    block = x_ref[...]
    gate_part = jnp.dot(block, gate_ref[...], preferred_element_type=jnp.float32)
    up_part = jnp.dot(block, up_ref[...], preferred_element_type=jnp.float32)
    hidden = (jax.nn.gelu(gate_part, approximate=True) * up_part).astype(jnp.bfloat16)
    part = jnp.dot(hidden, down_ref[...], preferred_element_type=jnp.float32)

    @pl.when(step == 0)
    def _():
        total[...] = part

    @pl.when(step > 0)
    def _():
        total[...] += part

    @pl.when(step == pl.num_programs(0) - 1)
    def _():
        out_ref[...] = total[...].astype(out_ref.dtype)


def feed_forward(block, w_gate, w_up, w_down):
    rows, width = block.shape
    units = w_gate.shape[1]
    tile = min(512, units)
    return pl.pallas_call(
        ffn_kernel,
        out_shape=jax.ShapeDtypeStruct(block.shape, jnp.bfloat16),
        grid=(units // tile,),
        in_specs=[
            pl.BlockSpec((rows, width), lambda i: (0, 0)),
            pl.BlockSpec((width, tile), lambda i: (0, i)),
            pl.BlockSpec((width, tile), lambda i: (0, i)),
            pl.BlockSpec((tile, width), lambda i: (i, 0)),
        ],
        out_specs=pl.BlockSpec((rows, width), lambda i: (0, 0)),
        scratch_shapes=[pltpu.VMEM((rows, width), jnp.float32)],
        compiler_params=pltpu.CompilerParams(vmem_limit_bytes=40 * 1024 * 1024),
        cost_estimate=pl.CostEstimate(
            flops=6 * rows * width * units,
            bytes_accessed=6 * width * units,
            transcendentals=rows * units,
        ),
    )(block, w_gate, w_up, w_down)


def per_device(
    hidden_in,
    layer_input,
    cached_len,
    page_table,
    kv_pool,
    norm_in,
    w_query,
    w_keyval,
    q_gain,
    k_gain,
    w_out,
    post_attn_gain,
    laurel_left,
    laurel_right,
    laurel_gain,
    pre_ffn_gain,
    w_gate,
    w_up,
    w_down,
    post_ffn_gain,
    ple_gate,
    ple_proj,
    ple_gain,
):
    dp_count = lax.axis_size("dp")
    tp_count = lax.axis_size("tensor")
    devices = dp_count * tp_count
    dp_at = lax.axis_index("dp")
    tp_at = lax.axis_index("tensor")
    chips = tp_count // 2
    chip_at = tp_at // 2
    core_at = tp_at % 2
    own_rows = hidden_in.shape[0]
    half_rows = own_rows // HALVES
    head_dim = q_gain.shape[0]
    local_heads = w_query.shape[1] // head_dim
    sharing = tp_count // KVH
    kv_head = tp_at // sharing
    slot_count = page_table.shape[1]
    page_len = kv_pool.shape[3]
    pool_dev = kv_pool.shape[0]
    needed = PROMPT_PAGES + REQ_DEV * (slot_count - PROMPT_PAGES)
    capacity = (needed + devices - 1) // devices
    page_count = (cached_len + page_len - 1) // page_len
    used_slots = jnp.arange(slot_count, dtype=jnp.int32)[None, :] < page_count[:, None]
    group_used = used_slots.reshape(dp_count, REQ_DEV * slot_count)
    group_table = page_table.reshape(dp_count, REQ_DEV * slot_count)
    own_flat = dp_at * tp_count + tp_at
    own_ids = own_flat * pool_dev + jnp.arange(pool_dev, dtype=jnp.int32)
    wanted = jnp.any(
        group_used[:, :, None] & (group_table[:, :, None] == own_ids[None, None, :]), axis=1
    )
    wanted_rank = jnp.cumsum(wanted.astype(jnp.int32), axis=1) - 1
    slot_ids = jnp.arange(capacity, dtype=jnp.int32)
    selector = (wanted[:, None, :] & (wanted_rank[:, None, :] == slot_ids[None, :, None])).astype(
        jnp.bfloat16
    )
    picked = jnp.einsum(
        "dcl,lkhpe->dhkcpe", selector, kv_pool, preferred_element_type=jnp.float32
    ).astype(jnp.bfloat16)
    outgoing = jnp.broadcast_to(
        picked[:, :, None],
        (dp_count, KVH, sharing // 2, 2, capacity, page_len, head_dim),
    ).reshape(devices, capacity, page_len, head_dim)
    near = spread_rows(hidden_in, tp_count)
    outgoing, *near = lax.optimization_barrier((outgoing, *near))
    arrived = lax.all_to_all(outgoing, ("dp", "tensor"), split_axis=0, concat_axis=0, tiled=True)
    own_used = lax.dynamic_index_in_dim(group_used, dp_at, 0, keepdims=False)
    own_table = lax.dynamic_index_in_dim(group_table, dp_at, 0, keepdims=False)
    every_page = jnp.arange(devices * pool_dev, dtype=jnp.int32)
    present = jnp.any(own_used[None, :] & (own_table[None, :] == every_page[:, None]), axis=1)
    present_rank = (
        jnp.cumsum(present.reshape(devices, pool_dev).astype(jnp.int32), axis=1) - 1
    ).reshape(-1)
    place = jnp.where(own_used, own_table // pool_dev * capacity + present_rank[own_table], 0)
    own_lengths = lax.dynamic_slice_in_dim(cached_len, dp_at * REQ_DEV, REQ_DEV, 0)
    near = jnp.stack(near)
    gathered = jnp.concatenate(
        [
            lax.dynamic_index_in_dim(
                near, (chip_at - t // 2 + chips) % chips * 2 + (core_at + t) % 2, 0, keepdims=False
            )
            for t in range(tp_count)
        ]
    )
    token_count = gathered.shape[0]
    new_count = token_count // REQ_DEV
    normed = norm_rows(gathered.astype(jnp.float32), norm_in).astype(jnp.bfloat16)
    offsets = jnp.arange(new_count, dtype=jnp.int32)
    position = (own_lengths[:, None] + offsets[None, :]).reshape(-1)
    queries = jnp.dot(normed, w_query, preferred_element_type=jnp.float32).reshape(
        token_count, local_heads, head_dim
    )
    queries = rotate(norm_rows(queries, q_gain), position).astype(jnp.bfloat16)
    key_weight = lax.dynamic_slice_in_dim(w_keyval, kv_head * head_dim, head_dim, 1)
    value_weight = lax.dynamic_slice_in_dim(w_keyval, (KVH + kv_head) * head_dim, head_dim, 1)
    fresh_keys = norm_rows(jnp.dot(normed, key_weight, preferred_element_type=jnp.float32), k_gain)
    fresh_keys = rotate(fresh_keys[:, None, :], position)[:, 0].astype(jnp.bfloat16)
    fresh_values = norm_rows(
        jnp.dot(normed, value_weight, preferred_element_type=jnp.float32), 1.0
    ).astype(jnp.bfloat16)
    fresh_keys = fresh_keys.reshape(REQ_DEV, new_count, head_dim)
    fresh_values = fresh_values.reshape(REQ_DEV, new_count, head_dim)
    by_half = (REQ_DEV, tp_count // REQ_DEV, HALVES, half_rows, local_heads * head_dim)
    arrived, queries, fresh_keys, fresh_values = lax.optimization_barrier(
        (arrived, queries, fresh_keys, fresh_values)
    )
    mine = arrived.reshape(devices * capacity, page_len, head_dim)
    other = swap_cores(mine, tp_count)
    queries = queries.reshape(by_half)
    offsets = offsets.reshape(by_half[1:4])

    own_x = hidden_in.astype(jnp.float32)
    own_normed = norm_rows(own_x, norm_in).astype(jnp.bfloat16)
    left_part = jnp.dot(own_normed, laurel_left, preferred_element_type=jnp.float32).astype(
        jnp.bfloat16
    )
    laurel_out = own_normed.astype(jnp.float32) + norm_rows(
        jnp.dot(left_part, laurel_right, preferred_element_type=jnp.float32), laurel_gain
    )
    beside = own_x + laurel_out

    owners = [
        (chip_at - step + chips) % chips * 2 + (core_at if same == 0 else 1 - core_at)
        for step in range(chips)
        for same in range(2)
    ]
    core_flag = core_at.reshape(1).astype(jnp.int32)
    width = hidden_in.shape[1]
    kept_rows, arriving = [], []
    for half in range(HALVES):
        half_queries = queries[:, :, half].reshape(REQ_DEV, new_count // HALVES, -1)
        if half:
            half_queries, sent = lax.optimization_barrier((half_queries, sent))
            arriving.append(send_chips(sent, tp_count))
        attended = attend(
            place,
            own_lengths,
            core_flag,
            half_queries,
            offsets[:, half].reshape(-1, 1),
            fresh_keys,
            fresh_values,
            mine,
            other,
        ).reshape(tp_count, half_rows, -1)
        if half:
            attended, *arriving[-1] = lax.optimization_barrier((attended, *arriving[-1]))
        attended = jnp.concatenate(
            [lax.dynamic_index_in_dim(attended, owner, 0, keepdims=False) for owner in owners]
        )
        partial = jnp.dot(attended, w_out, preferred_element_type=jnp.float32)
        joined, sent = join_cores(partial.reshape(chips, 2, half_rows, width), tp_count)
        kept_rows.append(joined[0])
        sent = sent[1:]
    arriving.append(send_chips(sent, tp_count))
    mixed_halves, entering, near_down = [], [], []
    for half in range(HALVES):
        rows = slice(half * half_rows, (half + 1) * half_rows)
        if half:
            near_down[-1], *arriving[half] = lax.optimization_barrier(
                (near_down[-1], *arriving[half])
            )
        projected = add_all(kept_rows[half], arriving[half])
        mixed_rows = (beside[rows] + norm_rows(projected, post_attn_gain)) * HALF_ROOT
        mixed_halves.append(mixed_rows)
        ffn_in = norm_rows(mixed_rows, pre_ffn_gain).astype(jnp.bfloat16)
        came = [shift_chips(ffn_in, tp_count, step) for step in range(1, chips)]
        entering.append((ffn_in, came))
        block = jnp.concatenate([ffn_in, swap_cores(ffn_in, tp_count)])
        near_down.append(feed_forward(block, w_gate, w_up, w_down))
    far_sent = []
    tie = near_down[-1]
    for half in range(HALVES):
        came = entering[half][1]
        tie, *came = lax.optimization_barrier((tie, *came))
        if half == 0:
            near_down[-1] = tie
        entering[half] = [piece for one in came for piece in (one, swap_cores(one, tp_count))]
    for half in range(HALVES):
        block = jnp.concatenate(entering[half])
        if half:
            block, far_sent[-1] = lax.optimization_barrier((block, far_sent[-1]))
        far_down = feed_forward(block, w_gate, w_up, w_down)
        far_sent.append(
            join_cores(far_down.reshape(chips - 1, 2, half_rows, width), tp_count)[1]
        )
    results = []
    for half in range(HALVES):
        rows = slice(half * half_rows, (half + 1) * half_rows)
        near_sum = join_cores(near_down[half].reshape(1, 2, half_rows, width), tp_count)[0][0]
        down = add_all(near_sum, send_chips(far_sent[half], tp_count))
        settled = mixed_halves[half] + norm_rows(down, post_ffn_gain)
        settled_half = settled.astype(jnp.bfloat16)
        gated = jax.nn.gelu(
            jnp.dot(settled_half, ple_gate, preferred_element_type=jnp.float32), approximate=True
        )
        gated = (gated * layer_input[rows].astype(jnp.float32)).astype(jnp.bfloat16)
        results.append(
            (
                settled
                + norm_rows(
                    jnp.dot(gated, ple_proj, preferred_element_type=jnp.float32), ple_gain
                )
            ).astype(jnp.bfloat16)
        )
    return jnp.concatenate(results, axis=0)


def solution(mesh):
    placed = (
        P(("dp", "tensor"), None),
        P(("dp", "tensor"), None),
        P(),
        P(),
        P(("dp", "tensor"), None, None, None, None),
        P(),
        P(None, "tensor"),
        P(),
        P(),
        P(),
        P("tensor", None),
        P(),
        P(),
        P(),
        P(),
        P(),
        P(None, "tensor"),
        P(None, "tensor"),
        P("tensor", None),
        P(),
        P(),
        P(),
        P(),
    )
    return jax.shard_map(
        per_device, mesh=mesh, in_specs=placed, out_specs=P(("dp", "tensor"), None), check_vma=False
    )
```
